256 devices in a mesh: row: 8 (over y, x_hi), col: 32 (over z, x_lo, core).
Axes of the slice: x: 4 (x_hi: 2, x_lo: 2; x = x_hi * 2 + x_lo), y: 4, z: 8, core: 2. Of those that a mesh axis runs over, the one named last changes fastest.
Arguments:
- inverses: bfloat16 [8, 128, 1024, 1024], P('row', 'col'), as said below
- coupling: bfloat16 [8, 128, 1024, 256], P('row', 'col'), may hold values from -0.1875 to 0.1875
- orders: int32 [8, 128], P('row', 'col'), may hold values from 512 to 1024, as said below
- owners: int32 [8, 128, 1], P(None, 'col'), may hold values from 0 to 7, as said below
- offsets: int32 [8, 128, 2], P(None, 'col'), may hold values from 0 to 2
- dense_slab: float32 [4096, 16384], P('row', 'col'), may hold values from -6 to 6
- pivots: float32 [1024], replicated, may hold values from 16 to 128
Outputs:
- result: float32 [4096, 16384], P('row', 'col')
The draws below stay inside these ranges and needn't reach their ends.
Inputs may be any that keep to these rules, and one draw needn't show every extreme that they name: `orders`: order of each subdomain; some subdomain has exactly 1024. `owners`: within the 4 subdomains of one device (entries r, s with the same r and the same s // 4) no row block is named twice. `inverses`: each inverse is symmetric.
All inputs are finite; a program needn't handle non-finite values.
Results may differ from the reference program's by a relative error of at most 0.0035.
Values may be sent and summed in bfloat16 or wider, within the bound.
No kernel may reach another device: no remote copies, remote signals or barrier semaphores. Data moves between devices by JAX's collectives and lax.ppermute only.
A program may use at most 64 MiB of HBM per device.

```python
import math
import jax
import jax.numpy as jnp
from jax import lax

ORD = 1024
KC = 256
TILE = 512
PW = 1024
SUBS = 4
NSUB_ROW = 128
OFF_UNIT = 128
ROWS = 4096
COLS = 16384
N_ROW = 8


def draw_inverses(key, part):
    shape = (N_ROW, NSUB_ROW, ORD, ORD)
    noise = jax.random.normal(key, shape, jnp.float32)
    symmetric = (noise + jnp.swapaxes(noise, 2, 3)) * (0.6 / ORD ** 0.5)
    identity = jnp.eye(ORD, dtype=jnp.float32)
    return (symmetric + identity).astype(jnp.bfloat16)


def draw_orders(key, part):
    values = jax.random.randint(key, (N_ROW, NSUB_ROW), ORD // 2, ORD + 1, jnp.int32)
    return values.at[0, 0].set(ORD)


def draw_owners(key, part):
    device_count = N_ROW * (NSUB_ROW // SUBS)
    device_keys = jax.random.split(jax.random.fold_in(key, 7), device_count)

    def pick(one_key):
        return jax.random.permutation(one_key, N_ROW)[:SUBS].astype(jnp.int32)
    chosen = jax.vmap(pick)(device_keys)
    return chosen.reshape(N_ROW, NSUB_ROW, 1)


def set_ends(array, rng, smallest, high):
    place = [jax.random.randint(jax.random.fold_in(rng, axis), (), 0, length) for axis, length in enumerate(array.shape)]
    widest = array.shape.index(max(array.shape))
    neighbour = place[:widest] + [(place[widest] + 1) % array.shape[widest]] + place[widest + 1:]
    return array.at[tuple(place)].set(smallest).at[tuple(neighbour)].set(high)


def levels(rng, dims, cuts, least, top_value):
    def one(dim, blocks):
        steps = jax.random.uniform(jax.random.fold_in(jax.random.fold_in(rng, 6), dim), (blocks,), jnp.float32, least / len(cuts), top_value / len(cuts))
        return jnp.repeat(jnp.exp(steps), dims[dim] // blocks).reshape((-1,) + (1,) * (len(dims) - dim - 1))

    loudness = one(*cuts[0])
    for cut in cuts[1:]:
        loudness = loudness * one(*cut)
    return loudness


def bell_draw(stream_key, shape, width, limit, shards=(), kind=jnp.bfloat16):
    entries = width * jax.random.normal(stream_key, shape, jnp.float32)
    if shards:
        entries = entries * levels(stream_key, shape, shards, -0.22, 0.18)
    return jnp.clip(entries, -limit, limit).astype(kind)


def setup_inputs(seed: int = 0) -> dict:
    seeds = jax.random.split(jax.random.key(seed), 8)
    return {
        "inverses": draw_inverses(jax.random.fold_in(seeds[7], 71), 0),
        "coupling": bell_draw(seeds[1], (N_ROW, NSUB_ROW, ORD, KC), ORD ** -0.5, 0.1875, ((0, 8), (1, 32))),
        "orders": draw_orders(jax.random.fold_in(seeds[7], 71), 0),
        "owners": draw_owners(jax.random.fold_in(seeds[7], 71), 0),
        "offsets": set_ends(jax.random.randint(seeds[4], (N_ROW, NSUB_ROW, 2), 0, 3), jax.random.fold_in(seeds[4], 1), 0, 2).astype(jnp.int32),
        "dense_slab": bell_draw(seeds[5], (ROWS, COLS), 1.0, 6.0, ((0, 8), (1, 32)), jnp.float32),
        "pivots": jnp.clip(jnp.exp(jax.random.uniform(seeds[6], (PW,), jnp.float32, math.log(16.0), math.log(128.0))), 16.0, 128.0),
    }


def make_tile(inverse, coupling_cols, order_size):
    live_rows = jnp.arange(inverse.shape[0], dtype=jnp.int32)[:, None] < order_size
    masked = jnp.where(live_rows, coupling_cols, jnp.zeros_like(coupling_cols))
    solved = jnp.dot(inverse.astype(jnp.float32), masked.astype(jnp.float32)).astype(jnp.bfloat16)
    return jnp.dot(masked.astype(jnp.float32).T, solved.astype(jnp.float32)).astype(jnp.bfloat16)


def reference(inverses, coupling, orders, owners, offsets, dense_slab, pivots):
    def add_one(counter, schur_sum):
        row_index = counter // NSUB_ROW
        sub_index = counter % NSUB_ROW
        tile_value = make_tile(inverses[row_index, sub_index], coupling[row_index, sub_index], orders[row_index, sub_index])
        row_start = (owners[row_index, sub_index, 0] * TILE + offsets[row_index, sub_index, 0] * OFF_UNIT).astype(jnp.int32)
        col_start = ((sub_index // SUBS) * TILE + offsets[row_index, sub_index, 1] * OFF_UNIT).astype(jnp.int32)
        current = lax.dynamic_slice(schur_sum, (row_start, col_start), (KC, KC))
        return lax.dynamic_update_slice(schur_sum, current + tile_value.astype(schur_sum.dtype), (row_start, col_start))

    schur_sum = lax.fori_loop(0, N_ROW * NSUB_ROW, add_one, jnp.zeros(dense_slab.shape, jnp.float32))
    updated = dense_slab - schur_sum
    panel = updated[:PW].astype(jnp.bfloat16)
    left_factor = (panel[:, :N_ROW * TILE].astype(jnp.float32) / pivots[:, None]).astype(jnp.bfloat16)
    return updated - jnp.dot(left_factor.astype(jnp.float32).T, panel.astype(jnp.float32))
```

```python
import jax
import jax.numpy as jnp
from jax import lax
from jax.experimental import pallas as pl
from jax.experimental.pallas import tpu as pltpu
from jax.sharding import PartitionSpec as P

BF = jnp.bfloat16
F32 = jnp.float32
ROWS = ("row", "col")
LIMIT = 48 * 1024 * 1024
OVER_ROWS = (((0,), (0,)), ((), ()))


def tile_kernel(orders, owners, inv_hbm, cpl_hbm, slab, panel_out, tiles_out, inv, cpl, inv_sem, cpl_sem):
    subs = inv_hbm.shape[0]
    me = lax.axis_index("row")
    for s in range(subs):
        pltpu.make_async_copy(cpl_hbm.at[s], cpl.at[s], cpl_sem.at[s]).start()
        pltpu.make_async_copy(inv_hbm.at[s], inv.at[s], inv_sem.at[s]).start()
    for d in range(8):
        for b in range(4):
            panel_out[d, b] = slab[b * 128 + d * 16:b * 128 + d * 16 + 16, :].astype(BF)
        panel_out[d, 4:6] = jnp.zeros((2, 16, 512), BF)
        tiles_out[d, 8:16] = jnp.zeros((8, 16, 512), BF)
    for s in range(subs):
        pltpu.make_async_copy(cpl_hbm.at[s], cpl.at[s], cpl_sem.at[s]).wait()
        pltpu.make_async_copy(inv_hbm.at[s], inv.at[s], inv_sem.at[s]).wait()
        live = lax.broadcasted_iota(jnp.int32, (1024, 256), 0) < orders[0, s]
        masked = jnp.where(live, cpl[s].astype(F32), 0.0).astype(BF)
        solved = jnp.dot(inv[s], masked, preferred_element_type=F32).astype(BF)
        tile = lax.dot_general(masked, solved, OVER_ROWS, preferred_element_type=F32).astype(BF)
        owner = owners[s, me]
        for k in range(8):
            tiles_out[owner, 8 + k, :, 0:256] = tile[k * 16:k * 16 + 16]
            tiles_out[owner, 8 + k, :, 256:512] = tile[128 + k * 16:144 + k * 16]

        @pl.when(owner < 2)
        def _():
            for d in range(8):
                panel_out[d, 4 + owner, :, 0:256] = tile[d * 16:d * 16 + 16]
                panel_out[d, 4 + owner, :, 256:512] = tile[128 + d * 16:144 + d * 16]


def panel_kernel(owners, offsets, piv, got, tiles_in, tiles_out, l0, l1, l2, l3, acc, piece, piv_cols, sems):
    del tiles_in
    me = lax.axis_index("row")
    piv_cols[...] = piv[...].T
    for o in range(2):
        for b in range(4):
            acc[o * 4 + b] = got[o, b].astype(F32)
    for src in range(8):
        for s in range(4):
            owner = owners[s, src]

            @pl.when(owner < 2)
            def _():
                block = owner * 4 + offsets[s, 0, src]
                cols = pl.ds(pl.multiple_of(offsets[s, 1, src] * 128, 128), 256)
                acc[block, :, cols] -= got[src, 4 + owner, :, 0:256].astype(F32)
                acc[block + 1, :, cols] -= got[src, 4 + owner, :, 256:512].astype(F32)
    piece[...] = acc[...].astype(BF)
    copies = [pltpu.make_async_copy(piece, tiles_out.at[d, 0:8], sems.at[d]) for d in range(8)]
    for copy in copies:
        copy.start()
    mine = piv_cols[pl.ds(pl.multiple_of(me * 16, 16), 16), :]
    for block in range(8):
        left = (piece[block].astype(F32) / mine[:, block:block + 1]).astype(BF)
        (l0, l1, l2, l3)[block // 2][block % 2] = left
    for copy in copies:
        copy.wait()


def take_quarter(total, left, panel, z_place, quarter):
    left_rows = left[...].reshape(256, 512)
    right = jnp.concatenate(
        [panel[z_place ^ mask, quarter * 2 + k] for mask in ORDER for k in range(2)], axis=0
    )
    return total - lax.dot_general(left_rows, right, OVER_ROWS, preferred_element_type=F32)


ORDER = (0, 2, 4, 6, 1, 3, 5, 7)


def first_kernel(owners, offsets, slab, got, left_a, left_b, out):
    me = lax.axis_index("row")
    col = lax.axis_index("col")
    z_place, quarter = col // 4, col % 4
    out[...] = slab[...]
    for src in range(8):
        for s in range(4):
            @pl.when(owners[s, src] == me)
            def _():
                row = pl.multiple_of(offsets[s, 0, src] * 128, 128)
                cols = pl.ds(pl.multiple_of(offsets[s, 1, src] * 128, 128), 256)
                block = got[src, 8:16].reshape(128, 512)
                out[pl.ds(row, 128), cols] -= block[:, 0:256].astype(F32)
                out[pl.ds(row + 128, 128), cols] -= block[:, 256:512].astype(F32)
    total = take_quarter(out[...], left_a, got, z_place, quarter)
    out[...] = take_quarter(total, left_b, got, z_place, quarter ^ 1)


def second_kernel(so_far, got, left_a, left_b, out):
    col = lax.axis_index("col")
    z_place, quarter = col // 4, col % 4
    total = take_quarter(so_far[...], left_a, got, z_place, quarter ^ 2)
    out[...] = take_quarter(total, left_b, got, z_place, quarter ^ 3)


def call(kernel, out_shape, in_specs, out_specs, scratch=(), flops=0, nbytes=0, aliases=None):
    return pl.pallas_call(
        kernel,
        out_shape=out_shape,
        in_specs=in_specs,
        out_specs=out_specs,
        scratch_shapes=list(scratch),
        input_output_aliases=aliases or {},
        compiler_params=pltpu.CompilerParams(vmem_limit_bytes=LIMIT),
        cost_estimate=pl.CostEstimate(flops=flops, bytes_accessed=nbytes, transcendentals=0),
    )


VM = pl.BlockSpec(memory_space=pltpu.VMEM)
SM = pl.BlockSpec(memory_space=pltpu.SMEM)
HB = pl.BlockSpec(memory_space=pl.ANY)


def shape(*dims, kind=BF):
    return jax.ShapeDtypeStruct(dims, kind)


def body(inverses, coupling, orders, owners, offsets, dense_slab, pivots):
    owner_rows = owners[:, :, 0].T
    offset_rows = offsets.transpose(1, 2, 0)
    panel_send, tiles_send = call(
        tile_kernel,
        (shape(8, 6, 16, 512), shape(8, 16, 16, 512)),
        [SM, SM, HB, HB, VM],
        (VM, VM),
        (
            pltpu.VMEM((4, 1024, 1024), BF),
            pltpu.VMEM((4, 1024, 256), BF),
            pltpu.SemaphoreType.DMA((4,)),
            pltpu.SemaphoreType.DMA((4,)),
        ),
        2_700_000_000,
        14_000_000,
    )(orders, owner_rows, inverses[0], coupling[0], dense_slab)
    panel_got = lax.all_to_all(panel_send, "row", 0, 0, tiled=True)
    tiles_send, l0, l1, l2, l3 = call(
        panel_kernel,
        (shape(8, 16, 16, 512),) + (shape(2, 16, 512),) * 4,
        [SM, SM, VM, VM, HB],
        (HB, VM, VM, VM, VM),
        (
            pltpu.VMEM((8, 16, 512), F32),
            pltpu.VMEM((8, 16, 512), BF),
            pltpu.VMEM((128, 8), F32),
            pltpu.SemaphoreType.DMA((8,)),
        ),
        1_000_000,
        2_000_000,
        {4: 0},
    )(owner_rows, offset_rows, pivots.reshape(8, 128), panel_got, tiles_send)

    def hop(piece, quarter):
        pairs = [(r * 32 + c, c * 32 + r * 4 + quarter) for r in range(8) for c in range(8)]
        return lax.ppermute(piece, ROWS, pairs)

    def over_col(value, mask):
        return lax.ppermute(value, "col", [(c, c ^ mask) for c in range(32)])

    hops = [hop(piece, quarter) for quarter, piece in enumerate((l0, l1, l2, l3))]
    own = (hops[0] + hops[1]) + (hops[2] + hops[3])
    tiles_send, own = lax.optimization_barrier((tiles_send, own))
    got = lax.all_to_all(tiles_send, "row", 0, 0, tiled=True)
    even = jnp.stack([own] + [over_col(own, 4 * k) for k in (2, 4, 6)])
    left_a = jnp.concatenate([even, over_col(even, 4)])
    left_b = over_col(left_a, 1)
    left_c = over_col(left_a, 2)
    left_d = over_col(left_c, 1)
    partial = call(
        first_kernel, shape(512, 512, kind=F32), [SM, SM, VM, VM, VM, VM], VM, (), 270_000_000, 5_000_000
    )(owner_rows, offset_rows, dense_slab, got, left_a, left_b)
    return call(
        second_kernel, shape(512, 512, kind=F32), [VM, VM, VM, VM], VM, (), 270_000_000, 4_000_000
    )(partial, got, left_c, left_d)


def solution(mesh):
    placed = (
        P("row", "col", None, None),
        P("row", "col", None, None),
        P("row", "col"),
        P(None, "col", None),
        P(None, "col", None),
        P("row", "col"),
        P(),
    )
    return jax.shard_map(
        body, mesh=mesh, in_specs=placed, out_specs=P("row", "col"), check_vma=False
    )
```

```python
import jax
import jax.numpy as jnp
from jax import lax
from jax.experimental import pallas as pl
from jax.experimental.pallas import tpu as pltpu
from jax.sharding import PartitionSpec as P

BF = jnp.bfloat16
F32 = jnp.float32
ROWS = ("row", "col")
LIMIT = 32 * 1024 * 1024
WHOLE = 60 * 1024 * 1024
OVER_ROWS = (((0,), (0,)), ((), ()))


def tile_kernel(orders, owners, inv_hbm, cpl_hbm, slab_hbm, send_hbm, keep, inv, cpl, slab, tiles, sems, out_sems):
    me = lax.axis_index("row")
    slab_copy = pltpu.make_async_copy(slab_hbm, slab, sems.at[8])
    cpl_copies = [pltpu.make_async_copy(cpl_hbm.at[s], cpl.at[s], sems.at[s]) for s in range(4)]
    inv_copies = [pltpu.make_async_copy(inv_hbm.at[s], inv.at[s], sems.at[4 + s]) for s in range(4)]
    cpl_copies[0].start()
    inv_copies[0].start()
    slab_copy.start()
    for s in range(1, 4):
        cpl_copies[s].start()
        inv_copies[s].start()
    slab_copy.wait()
    for y in range(4):
        for b in range(4):
            keep[y, b] = slab[b * 128 + y * 32:b * 128 + y * 32 + 32, :].astype(BF)
    copies = []
    for s in range(4):
        cpl_copies[s].wait()
        live = lax.broadcasted_iota(jnp.int32, (1024, 256), 0) < orders[0, s]
        masked = jnp.where(live, cpl[s], jnp.zeros((1024, 256), BF))
        inv_copies[s].wait()
        solved = lax.dot_general(masked, inv[s], OVER_ROWS, preferred_element_type=F32).astype(BF)
        tile = jnp.dot(solved, masked, preferred_element_type=F32).astype(BF)
        owner = owners[s, me]
        for k in range(8):
            tiles[s, k // 2, k % 2, :, 0:256] = tile[k * 16:k * 16 + 16]
            tiles[s, k // 2, k % 2, :, 256:512] = tile[128 + k * 16:144 + k * 16]
        copy = pltpu.make_async_copy(tiles.at[s], send_hbm.at[owner // 2, owner % 2, 1:5], out_sems.at[s])
        copy.start()
        copies.append(copy)
        panel_copy = pltpu.make_async_copy(tiles.at[s], send_hbm.at[:, owner % 2, 0], out_sems.at[4 + s])
        copies.append((owner, panel_copy))

        @pl.when(owner < 2)
        def _():
            panel_copy.start()

    for copy in copies:
        if isinstance(copy, tuple):
            pl.when(copy[0] < 2)(copy[1].wait)
        else:
            copy.wait()


def panel_kernel(owners, offsets, piv, got, keep, far_a, far_b, far_c, piece, left, acc, piv_cols):
    me = lax.axis_index("row")
    place = me // 2
    piv_cols[...] = piv[...].T

    @pl.when(place == 0)
    def _():
        acc[...] = keep[0].astype(F32)

    for y, far in enumerate((far_a, far_b, far_c)):
        @pl.when(place == y + 1)
        def _():
            acc[...] = far[...].astype(F32)

    for src in range(8):
        for s in range(4):
            @pl.when(owners[s, src] == me % 2)
            def _():
                block = offsets[s, 0, src]
                cols = pl.ds(pl.multiple_of(offsets[s, 1, src] * 128, 128), 256)
                rows = got[src, 0].reshape(32, 512).astype(F32)
                acc[block, :, cols] -= rows[:, 0:256]
                acc[block + 1, :, cols] -= rows[:, 256:512]
    piece[...] = acc[...].astype(BF)
    mine = piv_cols[pl.ds(pl.multiple_of(place * 32, 32), 32), :]
    first = me % 2 == 0
    for b in range(4):
        column = jnp.where(first, mine[:, b:b + 1], mine[:, 4 + b:5 + b])
        left[b] = (piece[b].astype(F32) / column).astype(BF)


def take(total, left, panel, mask):
    me = lax.axis_index("row")
    col = lax.axis_index("col")
    row = ((col // 4) & 4) | ((col & 3) ^ mask)
    right = jnp.concatenate([panel[row ^ me].reshape(128, 512), panel[row ^ me ^ 4].reshape(128, 512)], axis=0)
    return total - lax.dot_general(
        left[...].reshape(256, 512), right, OVER_ROWS, preferred_element_type=F32
    )


def base_kernel(owners, offsets, slab, tiles, out):
    me = lax.axis_index("row")
    out[...] = slab[...]
    for src in range(8):
        for s in range(4):
            @pl.when(owners[s, src] == me)
            def _():
                row = pl.multiple_of(offsets[s, 0, src] * 128, 128)
                cols = pl.ds(pl.multiple_of(offsets[s, 1, src] * 128, 128), 256)
                block = tiles[src, 1:5].reshape(128, 512)
                out[pl.ds(row, 128), cols] -= block[:, 0:256].astype(F32)
                out[pl.ds(row + 128, 128), cols] -= block[:, 256:512].astype(F32)


def middle_kernel(base, got, left_a, left_b, left_c, out):
    total = take(base[...], left_a, got, 0)
    out[...] = take(take(total, left_b, got, 1), left_c, got, 2)


def last_kernel(so_far, got, left, out):
    out[...] = take(so_far[...], left, got, 3)


def call(kernel, out_shape, in_specs, out_specs, scratch=(), flops=0, nbytes=0, aliases=None, limit=LIMIT):
    return pl.pallas_call(
        kernel,
        out_shape=out_shape,
        in_specs=in_specs,
        out_specs=out_specs,
        scratch_shapes=list(scratch),
        input_output_aliases=aliases or {},
        compiler_params=pltpu.CompilerParams(vmem_limit_bytes=limit),
        cost_estimate=pl.CostEstimate(flops=flops, bytes_accessed=nbytes, transcendentals=0),
    )


VM = pl.BlockSpec(memory_space=pltpu.VMEM)
SM = pl.BlockSpec(memory_space=pltpu.SMEM)
HB = pl.BlockSpec(memory_space=pltpu.HBM)


def shape(*dims, kind=BF):
    return jax.ShapeDtypeStruct(dims, kind)


def body(inverses, coupling, orders, owners, offsets, dense_slab, pivots):
    owner_rows = owners[:, :, 0].T
    offset_rows = offsets.transpose(1, 2, 0)
    send, keep = call(
        tile_kernel,
        (shape(4, 2, 5, 2, 16, 512), shape(4, 4, 32, 512)),
        [SM, SM, HB, HB, HB],
        (HB, VM),
        (
            pltpu.VMEM((4, 1024, 1024), BF),
            pltpu.VMEM((4, 1024, 256), BF),
            pltpu.VMEM((512, 512), F32),
            pltpu.VMEM((4, 4, 2, 16, 512), BF),
            pltpu.SemaphoreType.DMA((9,)),
            pltpu.SemaphoreType.DMA((8,)),
        ),
        2_700_000_000,
        14_000_000,
        limit=WHOLE,
    )(orders, owner_rows, inverses[0], coupling[0], dense_slab)
    tiles = lax.all_to_all(send.reshape(8, 5, 2, 16, 512), "row", 0, 0, tiled=True)
    far = [lax.ppermute(keep[k], "row", [(0, 2 * k), (1, 2 * k + 1)]) for k in range(1, 4)]
    piece, left = call(
        panel_kernel,
        (shape(4, 32, 512), shape(4, 32, 512)),
        [SM, SM] + [VM] * 6,
        (VM, VM),
        (pltpu.VMEM((4, 32, 512), F32), pltpu.VMEM((128, 8), F32)),
        1_000_000,
        2_000_000,
    )(owner_rows, offset_rows, pivots.reshape(8, 128), tiles, keep, *far)

    def hop(mask):
        pairs = [(r * 32 + c, c * 32 + (r ^ mask) * 4 + (r & 3)) for r in range(8) for c in range(8)]
        return lax.ppermute(left, ROWS, pairs)

    def spread(value, mask):
        return lax.ppermute(value, "col", [(z * 4 + (z & 3), (z ^ mask) * 4 + (z & 3)) for z in range(8)])

    def over_col(value, mask):
        return lax.ppermute(value, "col", [(c, c ^ mask) for c in range(32)])

    def over_row(value, mask):
        return lax.ppermute(value, "row", [(r, r ^ mask) for r in range(8)])

    pair = jnp.stack([hop(0), hop(4)])
    across = jnp.stack([piece, over_row(piece, 1)])
    got = jnp.concatenate([across] + [over_row(across, 2 * k) for k in range(1, 4)])
    left_a = (pair + spread(pair, 1)) + (spread(pair, 2) + spread(pair, 3))
    left_b = over_col(left_a, 1)
    left_c = over_col(left_a, 2)
    left_d = over_col(left_c, 1)
    full = shape(512, 512, kind=F32)
    base = call(base_kernel, full, [SM, SM, VM, VM], VM, (), 1_000_000, 3_000_000)(
        owner_rows, offset_rows, dense_slab, tiles
    )
    total = call(middle_kernel, full, [VM] * 5, VM, (), 400_000_000, 4_000_000)(base, got, left_a, left_b, left_c)
    return call(last_kernel, full, [VM] * 3, VM, (), 135_000_000, 3_000_000)(total, got, left_d)


def solution(mesh):
    placed = (
        P("row", "col", None, None),
        P("row", "col", None, None),
        P("row", "col"),
        P(None, "col", None),
        P(None, "col", None),
        P("row", "col"),
        P(),
    )
    return jax.shard_map(
        body, mesh=mesh, in_specs=placed, out_specs=P("row", "col"), check_vma=False
    )
```

```python
import jax
import jax.numpy as jnp
from jax import lax
from jax.experimental import pallas as pl
from jax.experimental.pallas import tpu as pltpu
from jax.sharding import PartitionSpec as P

BF = jnp.bfloat16
F32 = jnp.float32
ROWS = ("row", "col")
LIMIT = 32 * 1024 * 1024
WHOLE = 60 * 1024 * 1024
OVER_ROWS = (((0,), (0,)), ((), ()))


def tile_kernel(orders, owners, inv_hbm, cpl_hbm, slab_hbm, send_hbm, keep_b, keep_c, keep_d, inv, cpl, slab, slices, tiles, sems, out_sems):
    me = lax.axis_index("row")
    slab_copy = pltpu.make_async_copy(slab_hbm, slab, sems.at[8])
    cpl_copies = [pltpu.make_async_copy(cpl_hbm.at[s], cpl.at[s], sems.at[s]) for s in range(4)]
    inv_copies = [pltpu.make_async_copy(inv_hbm.at[s], inv.at[s], sems.at[4 + s]) for s in range(4)]
    cpl_copies[0].start()
    inv_copies[0].start()
    slab_copy.start()
    for s in range(1, 4):
        cpl_copies[s].start()
        inv_copies[s].start()
    slab_copy.wait()
    for y, keep in ((1, keep_b), (2, keep_c), (3, keep_d)):
        for b in range(4):
            keep[b] = slab[b * 128 + y * 32:b * 128 + y * 32 + 32, :].astype(BF)
    row = lax.broadcasted_iota(jnp.int32, (128, 128), 0)
    col = lax.broadcasted_iota(jnp.int32, (128, 128), 1)
    copies = []
    for s in range(4):
        cpl_copies[s].wait()
        live = lax.broadcasted_iota(jnp.int32, (1024, 256), 0) < orders[0, s]
        masked = jnp.where(live, cpl[s], jnp.zeros((1024, 256), BF))
        inv_copies[s].wait()
        solved = lax.dot_general(masked, inv[s], OVER_ROWS, preferred_element_type=F32).astype(BF)
        tile = jnp.dot(solved, masked, preferred_element_type=F32)
        owner = owners[s, me]
        second = tile[128:, 128:]
        packed = jnp.where(row <= col, tile[:128, :128], second).astype(BF)
        diagonal = jnp.sum(jnp.where(row == col, second, 0.0), axis=0, keepdims=True)
        tile = tile.astype(BF)
        for k in range(8):
            tiles[s, k] = packed[k * 16:k * 16 + 16]
            tiles[s, 8 + k] = tile[k * 16:k * 16 + 16, 128:]
        tiles[s, 16] = jnp.broadcast_to(diagonal, (16, 128)).astype(BF)
        for half in range(2):
            for k in range(8):
                for side in range(2):
                    slices[s, k // 2, half * 4 + side * 2 + k % 2] = tile[
                        half * 128 + k * 16:half * 128 + k * 16 + 16, side * 128:side * 128 + 128
                    ]
        copy = pltpu.make_async_copy(tiles.at[s], send_hbm.at[owner // 2, owner % 2, 8:25], out_sems.at[s])
        copy.start()
        copies.append(copy)
        panel_copy = pltpu.make_async_copy(slices.at[s], send_hbm.at[:, owner % 2, 0:8], out_sems.at[4 + s])
        copies.append((owner, panel_copy))

        @pl.when(owner < 2)
        def _():
            panel_copy.start()

    for copy in copies:
        if isinstance(copy, tuple):
            pl.when(copy[0] < 2)(copy[1].wait)
        else:
            copy.wait()


def panel_kernel(owners, offsets, piv, got, slab, far_a, far_b, far_c, piece, left, acc, piv_cols):
    me = lax.axis_index("row")
    place = me // 2
    piv_cols[...] = piv[...].T

    @pl.when(place == 0)
    def _():
        for b in range(4):
            acc[b] = slab[b * 128:b * 128 + 32, :]

    for y, far in ((1, far_a), (2, far_b), (3, far_c)):
        @pl.when(place == y)
        def _():
            acc[...] = far[...].astype(F32)

    for src in range(8):
        for s in range(4):
            @pl.when(owners[s, src] == me % 2)
            def _():
                block = offsets[s, 0, src]
                for half in range(2):
                    for side in range(2):
                        cols = pl.ds(pl.multiple_of((offsets[s, 1, src] + side) * 128, 128), 128)
                        unit = half * 4 + side * 2
                        acc[block + half, :, cols] -= got[src, unit:unit + 2].reshape(32, 128).astype(F32)
    piece[...] = acc[...].astype(BF)
    mine = piv_cols[pl.ds(pl.multiple_of(place * 32, 32), 32), :]
    first = me % 2 == 0
    for b in range(4):
        column = jnp.where(first, mine[:, b:b + 1], mine[:, 4 + b:5 + b])
        left[b] = (piece[b].astype(F32) / column).astype(BF)


def take(total, left, panel, mask):
    me = lax.axis_index("row")
    col = lax.axis_index("col")
    row = ((col // 4) & 4) | ((col & 3) ^ mask)
    right = jnp.concatenate([panel[row ^ me].reshape(128, 512), panel[row ^ me ^ 4].reshape(128, 512)], axis=0)
    return total - lax.dot_general(
        left[...].reshape(256, 512), right, OVER_ROWS, preferred_element_type=F32
    )


def base_kernel(owners, offsets, slab, tiles, out):
    me = lax.axis_index("row")
    row = lax.broadcasted_iota(jnp.int32, (128, 128), 0)
    col = lax.broadcasted_iota(jnp.int32, (128, 128), 1)
    out[...] = slab[...]
    for src in range(8):
        for s in range(4):
            @pl.when(owners[s, src] == me)
            def _():
                top = pl.multiple_of(offsets[s, 0, src] * 128, 128)
                start = pl.multiple_of(offsets[s, 1, src] * 128, 128)
                upper, lower = pl.ds(top, 128), pl.ds(top + 128, 128)
                first, second = pl.ds(start, 128), pl.ds(start + 128, 128)
                packed = tiles[src, 8:16].reshape(128, 128).astype(F32)
                right = tiles[src, 16:24].reshape(128, 128).astype(F32)
                diagonal = tiles[src, 24].astype(F32)[0:1, :]
                turned = packed.T
                out[upper, first] -= jnp.where(row <= col, packed, turned)
                out[upper, second] -= right
                out[lower, first] -= right.T
                out[lower, second] -= jnp.where(row > col, packed, jnp.where(row < col, turned, diagonal))


def middle_kernel(base, got, left_a, left_b, left_c, out):
    total = take(base[...], left_a, got, 0)
    out[...] = take(take(total, left_b, got, 1), left_c, got, 2)


def last_kernel(so_far, got, left, out):
    out[...] = take(so_far[...], left, got, 3)


def call(kernel, out_shape, in_specs, out_specs, scratch=(), flops=0, nbytes=0, aliases=None, limit=LIMIT):
    return pl.pallas_call(
        kernel,
        out_shape=out_shape,
        in_specs=in_specs,
        out_specs=out_specs,
        scratch_shapes=list(scratch),
        input_output_aliases=aliases or {},
        compiler_params=pltpu.CompilerParams(vmem_limit_bytes=limit),
        cost_estimate=pl.CostEstimate(flops=flops, bytes_accessed=nbytes, transcendentals=0),
    )


VM = pl.BlockSpec(memory_space=pltpu.VMEM)
SM = pl.BlockSpec(memory_space=pltpu.SMEM)
HB = pl.BlockSpec(memory_space=pltpu.HBM)


def shape(*dims, kind=BF):
    return jax.ShapeDtypeStruct(dims, kind)


def body(inverses, coupling, orders, owners, offsets, dense_slab, pivots):
    owner_rows = owners[:, :, 0].T
    offset_rows = offsets.transpose(1, 2, 0)
    send, *keep = call(
        tile_kernel,
        (shape(4, 2, 25, 16, 128),) + (shape(4, 32, 512),) * 3,
        [SM, SM, HB, HB, HB],
        (HB, VM, VM, VM),
        (
            pltpu.VMEM((4, 1024, 1024), BF),
            pltpu.VMEM((4, 1024, 256), BF),
            pltpu.VMEM((512, 512), F32),
            pltpu.VMEM((4, 4, 8, 16, 128), BF),
            pltpu.VMEM((4, 17, 16, 128), BF),
            pltpu.SemaphoreType.DMA((9,)),
            pltpu.SemaphoreType.DMA((8,)),
        ),
        2_700_000_000,
        14_000_000,
        limit=WHOLE,
    )(orders, owner_rows, inverses[0], coupling[0], dense_slab)
    tiles = lax.all_to_all(send.reshape(8, 25, 16, 128), "row", 0, 0, tiled=True)
    far = [lax.ppermute(keep[k - 1], "row", [(0, 2 * k), (1, 2 * k + 1)]) for k in range(1, 4)]
    piece, left = call(
        panel_kernel,
        (shape(4, 32, 512), shape(4, 32, 512)),
        [SM, SM] + [VM] * 6,
        (VM, VM),
        (pltpu.VMEM((4, 32, 512), F32), pltpu.VMEM((128, 8), F32)),
        1_000_000,
        2_000_000,
    )(owner_rows, offset_rows, pivots.reshape(8, 128), tiles, dense_slab, *far)

    def hop(mask):
        pairs = [(r * 32 + c, c * 32 + (r ^ mask) * 4 + (r & 3)) for r in range(8) for c in range(8)]
        return lax.ppermute(left, ROWS, pairs)

    def spread(value, mask):
        return lax.ppermute(value, "col", [(z * 4 + (z & 3), (z ^ mask) * 4 + (z & 3)) for z in range(8)])

    def over_col(value, mask):
        return lax.ppermute(value, "col", [(c, c ^ mask) for c in range(32)])

    def over_row(value, mask):
        return lax.ppermute(value, "row", [(r, r ^ mask) for r in range(8)])

    pair = jnp.stack([hop(0), hop(4)])
    across = jnp.stack([piece, over_row(piece, 1)])
    got = jnp.concatenate([across] + [over_row(across, 2 * k) for k in range(1, 4)])
    left_a = (pair + spread(pair, 1)) + (spread(pair, 2) + spread(pair, 3))
    left_b = over_col(left_a, 1)
    left_c = over_col(left_a, 2)
    left_d = over_col(left_c, 1)
    full = shape(512, 512, kind=F32)
    base = call(base_kernel, full, [SM, SM, VM, VM], VM, (), 1_000_000, 3_000_000)(
        owner_rows, offset_rows, dense_slab, tiles
    )
    total = call(middle_kernel, full, [VM] * 5, VM, (), 400_000_000, 4_000_000)(base, got, left_a, left_b, left_c)
    return call(last_kernel, full, [VM] * 3, VM, (), 135_000_000, 3_000_000)(total, got, left_d)


def solution(mesh):
    placed = (
        P("row", "col", None, None),
        P("row", "col", None, None),
        P("row", "col"),
        P(None, "col", None),
        P(None, "col", None),
        P("row", "col"),
        P(),
    )
    return jax.shard_map(
        body, mesh=mesh, in_specs=placed, out_specs=P("row", "col"), check_vma=False
    )
```

```python
import jax
import jax.numpy as jnp
from jax import lax
from jax.experimental import pallas as pl
from jax.experimental.pallas import tpu as pltpu
from jax.sharding import PartitionSpec as P

BF = jnp.bfloat16
F32 = jnp.float32
ROWS = ("row", "col")
LIMIT = 32 * 1024 * 1024
WHOLE = 60 * 1024 * 1024
OVER_ROWS = (((0,), (0,)), ((), ()))


def tile_kernel(orders, owners, inv_hbm, cpl_hbm, slab_hbm, send_hbm, keep_b, keep_c, keep_d, inv, cpl, slab, slices, tiles, sems, out_sems):
    me = lax.axis_index("row")
    slab_copy = pltpu.make_async_copy(slab_hbm, slab, sems.at[8])
    cpl_copies = [pltpu.make_async_copy(cpl_hbm.at[s], cpl.at[s], sems.at[s]) for s in range(4)]
    inv_copies = [pltpu.make_async_copy(inv_hbm.at[s], inv.at[s], sems.at[4 + s]) for s in range(4)]
    cpl_copies[0].start()
    inv_copies[0].start()
    for s in range(1, 4):
        cpl_copies[s].start()
        inv_copies[s].start()
    slab_copy.start()
    row = lax.broadcasted_iota(jnp.int32, (128, 128), 0)
    col = lax.broadcasted_iota(jnp.int32, (128, 128), 1)
    copies = []
    for s in range(4):
        cpl_copies[s].wait()
        live = lax.broadcasted_iota(jnp.int32, (1024, 256), 0) < orders[0, s]
        masked = jnp.where(live, cpl[s], jnp.zeros((1024, 256), BF))
        inv_copies[s].wait()
        solved = lax.dot_general(masked, inv[s], OVER_ROWS, preferred_element_type=F32).astype(BF)
        tile = jnp.dot(solved, masked, preferred_element_type=F32)
        owner = owners[s, me]
        second = tile[128:, 128:]
        packed = jnp.where(row <= col, tile[:128, :128], second).astype(BF)
        diagonal = jnp.sum(jnp.where(row == col, second, 0.0), axis=0, keepdims=True)
        tile = tile.astype(BF)
        for k in range(8):
            tiles[s, k] = packed[k * 16:k * 16 + 16]
            tiles[s, 8 + k] = tile[k * 16:k * 16 + 16, 128:]
        tiles[s, 16] = jnp.broadcast_to(diagonal, (16, 128)).astype(BF)
        for half in range(2):
            for k in range(8):
                for side in range(2):
                    slices[s, k // 2, half * 4 + side * 2 + k % 2] = tile[
                        half * 128 + k * 16:half * 128 + k * 16 + 16, side * 128:side * 128 + 128
                    ]
        copy = pltpu.make_async_copy(tiles.at[s], send_hbm.at[owner // 2, owner % 2, 8:25], out_sems.at[s])
        copy.start()
        copies.append(copy)
        panel_copy = pltpu.make_async_copy(slices.at[s], send_hbm.at[:, owner % 2, 0:8], out_sems.at[4 + s])
        copies.append((owner, panel_copy))

        @pl.when(owner < 2)
        def _():
            panel_copy.start()

    slab_copy.wait()
    for y, keep in ((1, keep_b), (2, keep_c), (3, keep_d)):
        for b in range(4):
            keep[b] = slab[b * 128 + y * 32:b * 128 + y * 32 + 32, :].astype(BF)
    for copy in copies:
        if isinstance(copy, tuple):
            pl.when(copy[0] < 2)(copy[1].wait)
        else:
            copy.wait()


def panel_kernel(owners, offsets, piv, got, slab, far_a, far_b, far_c, piece, left, acc, piv_cols):
    me = lax.axis_index("row")
    place = me // 2
    piv_cols[...] = piv[...].T

    @pl.when(place == 0)
    def _():
        for b in range(4):
            acc[b] = slab[b * 128:b * 128 + 32, :]

    for y, far in ((1, far_a), (2, far_b), (3, far_c)):
        @pl.when(place == y)
        def _():
            acc[...] = far[...].astype(F32)

    for src in range(8):
        for s in range(4):
            @pl.when(owners[s, src] == me % 2)
            def _():
                block = offsets[s, 0, src]
                for half in range(2):
                    for side in range(2):
                        cols = pl.ds(pl.multiple_of((offsets[s, 1, src] + side) * 128, 128), 128)
                        unit = half * 4 + side * 2
                        acc[block + half, :, cols] -= got[src, unit:unit + 2].reshape(32, 128).astype(F32)
    piece[...] = acc[...].astype(BF)
    mine = piv_cols[pl.ds(pl.multiple_of(place * 32, 32), 32), :]
    first = me % 2 == 0
    for b in range(4):
        column = jnp.where(first, mine[:, b:b + 1], mine[:, 4 + b:5 + b])
        left[b] = (piece[b].astype(F32) / column).astype(BF)


def take(total, left, panel, mask):
    me = lax.axis_index("row")
    col = lax.axis_index("col")
    row = ((col // 4) & 4) | ((col & 3) ^ mask)
    right = jnp.concatenate([panel[row ^ me].reshape(128, 512), panel[row ^ me ^ 4].reshape(128, 512)], axis=0)
    return total - lax.dot_general(
        left[...].reshape(256, 512), right, OVER_ROWS, preferred_element_type=F32
    )


def base_kernel(owners, offsets, slab, tiles, out):
    me = lax.axis_index("row")
    row = lax.broadcasted_iota(jnp.int32, (128, 128), 0)
    col = lax.broadcasted_iota(jnp.int32, (128, 128), 1)
    out[...] = slab[...]
    for src in range(8):
        for s in range(4):
            @pl.when(owners[s, src] == me)
            def _():
                top = pl.multiple_of(offsets[s, 0, src] * 128, 128)
                start = pl.multiple_of(offsets[s, 1, src] * 128, 128)
                upper, lower = pl.ds(top, 128), pl.ds(top + 128, 128)
                first, second = pl.ds(start, 128), pl.ds(start + 128, 128)
                packed = tiles[src, 8:16].reshape(128, 128).astype(F32)
                right = tiles[src, 16:24].reshape(128, 128).astype(F32)
                diagonal = tiles[src, 24].astype(F32)[0:1, :]
                turned = packed.T
                out[upper, first] -= jnp.where(row <= col, packed, turned)
                out[upper, second] -= right
                out[lower, first] -= right.T
                out[lower, second] -= jnp.where(row > col, packed, jnp.where(row < col, turned, diagonal))


def middle_kernel(base, got, left_a, left_b, left_c, out):
    total = take(base[...], left_a, got, 0)
    out[...] = take(take(total, left_b, got, 1), left_c, got, 2)


def last_kernel(so_far, got, left, out):
    out[...] = take(so_far[...], left, got, 3)


def call(kernel, out_shape, in_specs, out_specs, scratch=(), flops=0, nbytes=0, aliases=None, limit=LIMIT):
    return pl.pallas_call(
        kernel,
        out_shape=out_shape,
        in_specs=in_specs,
        out_specs=out_specs,
        scratch_shapes=list(scratch),
        input_output_aliases=aliases or {},
        compiler_params=pltpu.CompilerParams(vmem_limit_bytes=limit),
        cost_estimate=pl.CostEstimate(flops=flops, bytes_accessed=nbytes, transcendentals=0),
    )


VM = pl.BlockSpec(memory_space=pltpu.VMEM)
SM = pl.BlockSpec(memory_space=pltpu.SMEM)
HB = pl.BlockSpec(memory_space=pltpu.HBM)


def shape(*dims, kind=BF):
    return jax.ShapeDtypeStruct(dims, kind)


def body(inverses, coupling, orders, owners, offsets, dense_slab, pivots):
    owner_rows = owners[:, :, 0].T
    offset_rows = offsets.transpose(1, 2, 0)
    send, *keep = call(
        tile_kernel,
        (shape(4, 2, 25, 16, 128),) + (shape(4, 32, 512),) * 3,
        [SM, SM, HB, HB, HB],
        (HB, VM, VM, VM),
        (
            pltpu.VMEM((4, 1024, 1024), BF),
            pltpu.VMEM((4, 1024, 256), BF),
            pltpu.VMEM((512, 512), F32),
            pltpu.VMEM((4, 4, 8, 16, 128), BF),
            pltpu.VMEM((4, 17, 16, 128), BF),
            pltpu.SemaphoreType.DMA((9,)),
            pltpu.SemaphoreType.DMA((8,)),
        ),
        2_700_000_000,
        14_000_000,
        limit=WHOLE,
    )(orders, owner_rows, inverses[0], coupling[0], dense_slab)
    tiles = lax.all_to_all(send.reshape(8, 25, 16, 128), "row", 0, 0, tiled=True)
    far = [lax.ppermute(keep[k - 1], "row", [(0, 2 * k), (1, 2 * k + 1)]) for k in range(1, 4)]
    piece, left = call(
        panel_kernel,
        (shape(4, 32, 512), shape(4, 32, 512)),
        [SM, SM] + [VM] * 6,
        (VM, VM),
        (pltpu.VMEM((4, 32, 512), F32), pltpu.VMEM((128, 8), F32)),
        1_000_000,
        2_000_000,
    )(owner_rows, offset_rows, pivots.reshape(8, 128), tiles, dense_slab, *far)

    def hop(mask):
        pairs = [(r * 32 + c, c * 32 + (r ^ mask) * 4 + (r & 3)) for r in range(8) for c in range(8)]
        return lax.ppermute(left, ROWS, pairs)

    def spread(value, mask):
        return lax.ppermute(value, "col", [(z * 4 + (z & 3), (z ^ mask) * 4 + (z & 3)) for z in range(8)])

    def over_col(value, mask):
        return lax.ppermute(value, "col", [(c, c ^ mask) for c in range(32)])

    def over_row(value, mask):
        return lax.ppermute(value, "row", [(r, r ^ mask) for r in range(8)])

    pair = jnp.stack([hop(0), hop(4)])
    across = jnp.stack([piece, over_row(piece, 1)])
    got = jnp.concatenate([across] + [over_row(across, 2 * k) for k in range(1, 4)])
    left_a = (pair + spread(pair, 1)) + (spread(pair, 2) + spread(pair, 3))
    left_b = over_col(left_a, 1)
    left_c = over_col(left_a, 2)
    left_d = over_col(left_c, 1)
    full = shape(512, 512, kind=F32)
    base = call(base_kernel, full, [SM, SM, VM, VM], VM, (), 1_000_000, 3_000_000)(
        owner_rows, offset_rows, dense_slab, tiles
    )
    total = call(middle_kernel, full, [VM] * 5, VM, (), 400_000_000, 4_000_000)(base, got, left_a, left_b, left_c)
    return call(last_kernel, full, [VM] * 3, VM, (), 135_000_000, 3_000_000)(total, got, left_d)


def solution(mesh):
    placed = (
        P("row", "col", None, None),
        P("row", "col", None, None),
        P("row", "col"),
        P(None, "col", None),
        P(None, "col", None),
        P("row", "col"),
        P(),
    )
    return jax.shard_map(
        body, mesh=mesh, in_specs=placed, out_specs=P("row", "col"), check_vma=False
    )
```

```python
import jax
import jax.numpy as jnp
from jax import lax
from jax.experimental import pallas as pl
from jax.experimental.pallas import tpu as pltpu
from jax.sharding import PartitionSpec as P

BF = jnp.bfloat16
F32 = jnp.float32
ROWS = ("row", "col")
LIMIT = 32 * 1024 * 1024
WHOLE = 60 * 1024 * 1024
OVER_ROWS = (((0,), (0,)), ((), ()))


def tile_kernel(orders, owners, inv_hbm, cpl_hbm, slab_hbm, send_hbm, keep_b, keep_c, keep_d, inv, cpl, slab, slices, tiles, sems, out_sems):
    me = lax.axis_index("row")
    slab_copy = pltpu.make_async_copy(slab_hbm, slab, sems.at[8])
    cpl_copies = [pltpu.make_async_copy(cpl_hbm.at[s], cpl.at[s], sems.at[s]) for s in range(4)]
    inv_copies = [pltpu.make_async_copy(inv_hbm.at[s], inv.at[s], sems.at[4 + s]) for s in range(4)]
    cpl_copies[0].start()
    inv_copies[0].start()
    for s in range(1, 4):
        cpl_copies[s].start()
        inv_copies[s].start()
    slab_copy.start()
    row = lax.broadcasted_iota(jnp.int32, (128, 128), 0)
    col = lax.broadcasted_iota(jnp.int32, (128, 128), 1)
    copies = []
    for s in range(4):
        cpl_copies[s].wait()
        live = lax.broadcasted_iota(jnp.int32, (1024, 256), 0) < orders[0, s]
        masked = jnp.where(live, cpl[s], jnp.zeros((1024, 256), BF))
        inv_copies[s].wait()
        solved = lax.dot_general(masked, inv[s], OVER_ROWS, preferred_element_type=F32).astype(BF)
        tile = jnp.dot(solved, masked, preferred_element_type=F32)
        owner = owners[s, me]
        second = tile[128:, 128:]
        packed = jnp.where(row <= col, tile[:128, :128], second).astype(BF)
        diagonal = jnp.sum(jnp.where(row == col, second, 0.0), axis=0, keepdims=True)
        tile = tile.astype(BF)
        for k in range(8):
            tiles[s, k] = packed[k * 16:k * 16 + 16]
            tiles[s, 8 + k] = tile[k * 16:k * 16 + 16, 128:]
        tiles[s, 16] = jnp.broadcast_to(diagonal, (16, 128)).astype(BF)
        for half in range(2):
            for k in range(8):
                for side in range(2):
                    slices[s, k // 2, half * 4 + side * 2 + k % 2] = tile[
                        half * 128 + k * 16:half * 128 + k * 16 + 16, side * 128:side * 128 + 128
                    ]
        copy = pltpu.make_async_copy(tiles.at[s], send_hbm.at[owner // 2, owner % 2, 8:25], out_sems.at[s])
        copy.start()
        copies.append(copy)
        panel_copy = pltpu.make_async_copy(slices.at[s], send_hbm.at[:, owner % 2, 0:8], out_sems.at[4 + s])
        copies.append((owner, panel_copy))

        @pl.when(owner < 2)
        def _():
            panel_copy.start()

    slab_copy.wait()
    for y, keep in ((1, keep_b), (2, keep_c), (3, keep_d)):
        for b in range(4):
            keep[b] = slab[b * 128 + y * 32:b * 128 + y * 32 + 32, :].astype(BF)
    for copy in copies:
        if isinstance(copy, tuple):
            pl.when(copy[0] < 2)(copy[1].wait)
        else:
            copy.wait()


def panel_kernel(owners, offsets, piv, got, slab, far_a, far_b, far_c, piece, left, acc, piv_cols):
    me = lax.axis_index("row")
    place = me // 2
    piv_cols[...] = piv[...].T

    @pl.when(place == 0)
    def _():
        for b in range(4):
            acc[b] = slab[b * 128:b * 128 + 32, :]

    for y, far in ((1, far_a), (2, far_b), (3, far_c)):
        @pl.when(place == y)
        def _():
            acc[...] = far[...].astype(F32)

    for src in range(8):
        for s in range(4):
            @pl.when(owners[s, src] == me % 2)
            def _():
                block = offsets[s, 0, src]
                for half in range(2):
                    for side in range(2):
                        cols = pl.ds(pl.multiple_of((offsets[s, 1, src] + side) * 128, 128), 128)
                        unit = half * 4 + side * 2
                        acc[block + half, :, cols] -= got[src, unit:unit + 2].reshape(32, 128).astype(F32)
    piece[...] = acc[...].astype(BF)
    mine = piv_cols[pl.ds(pl.multiple_of(place * 32, 32), 32), :]
    first = me % 2 == 0
    for b in range(4):
        column = jnp.where(first, mine[:, b:b + 1], mine[:, 4 + b:5 + b])
        left[b] = (piece[b].astype(F32) / column).astype(BF)


def take(total, left, panel, mask):
    me = lax.axis_index("row")
    col = lax.axis_index("col")
    row = ((col // 4) & 4) | ((col & 3) ^ mask)
    right = jnp.concatenate([panel[row ^ me].reshape(128, 512), panel[row ^ me ^ 4].reshape(128, 512)], axis=0)
    return total - lax.dot_general(
        left[...].reshape(256, left.shape[-1]), right, OVER_ROWS, preferred_element_type=F32
    )


def base_kernel(owners, offsets, slab, tiles, out):
    me = lax.axis_index("row")
    row = lax.broadcasted_iota(jnp.int32, (128, 128), 0)
    col = lax.broadcasted_iota(jnp.int32, (128, 128), 1)
    out[...] = slab[...]
    for src in range(8):
        for s in range(4):
            @pl.when(owners[s, src] == me)
            def _():
                top = pl.multiple_of(offsets[s, 0, src] * 128, 128)
                start = pl.multiple_of(offsets[s, 1, src] * 128, 128)
                upper, lower = pl.ds(top, 128), pl.ds(top + 128, 128)
                first, second = pl.ds(start, 128), pl.ds(start + 128, 128)
                packed = tiles[src, 8:16].reshape(128, 128).astype(F32)
                right = tiles[src, 16:24].reshape(128, 128).astype(F32)
                diagonal = tiles[src, 24].astype(F32)[0:1, :]
                turned = packed.T
                out[upper, first] -= jnp.where(row <= col, packed, turned)
                out[upper, second] -= right
                out[lower, first] -= right.T
                out[lower, second] -= jnp.where(row > col, packed, jnp.where(row < col, turned, diagonal))


def middle_kernel(base, got, left_a, left_b, left_c, out):
    total = take(base[...], left_a, got, 0)
    out[...] = take(take(total, left_b, got, 1), left_c, got, 2)


def last_kernel(so_far, panel, left, out_hbm, total, sems):
    copies = []
    for part in range(4):
        rows = slice(part * 128, part * 128 + 128)
        total[rows] = take(so_far[rows], left[:, :, :, rows], panel, 3)
        copies.append(pltpu.make_async_copy(total.at[rows], out_hbm.at[rows], sems.at[part]))
        copies[-1].start()
    for copy in copies:
        copy.wait()


def call(kernel, out_shape, in_specs, out_specs, scratch=(), flops=0, nbytes=0, aliases=None, limit=LIMIT):
    return pl.pallas_call(
        kernel,
        out_shape=out_shape,
        in_specs=in_specs,
        out_specs=out_specs,
        scratch_shapes=list(scratch),
        input_output_aliases=aliases or {},
        compiler_params=pltpu.CompilerParams(vmem_limit_bytes=limit),
        cost_estimate=pl.CostEstimate(flops=flops, bytes_accessed=nbytes, transcendentals=0),
    )


VM = pl.BlockSpec(memory_space=pltpu.VMEM)
SM = pl.BlockSpec(memory_space=pltpu.SMEM)
HB = pl.BlockSpec(memory_space=pltpu.HBM)


def shape(*dims, kind=BF):
    return jax.ShapeDtypeStruct(dims, kind)


def body(inverses, coupling, orders, owners, offsets, dense_slab, pivots):
    owner_rows = owners[:, :, 0].T
    offset_rows = offsets.transpose(1, 2, 0)
    send, *keep = call(
        tile_kernel,
        (shape(4, 2, 25, 16, 128),) + (shape(4, 32, 512),) * 3,
        [SM, SM, HB, HB, HB],
        (HB, VM, VM, VM),
        (
            pltpu.VMEM((4, 1024, 1024), BF),
            pltpu.VMEM((4, 1024, 256), BF),
            pltpu.VMEM((512, 512), F32),
            pltpu.VMEM((4, 4, 8, 16, 128), BF),
            pltpu.VMEM((4, 17, 16, 128), BF),
            pltpu.SemaphoreType.DMA((9,)),
            pltpu.SemaphoreType.DMA((8,)),
        ),
        2_700_000_000,
        14_000_000,
        limit=WHOLE,
    )(orders, owner_rows, inverses[0], coupling[0], dense_slab)
    tiles = lax.all_to_all(send.reshape(8, 25, 16, 128), "row", 0, 0, tiled=True)
    far = [lax.ppermute(keep[k - 1], "row", [(0, 2 * k), (1, 2 * k + 1)]) for k in range(1, 4)]
    piece, left = call(
        panel_kernel,
        (shape(4, 32, 512), shape(4, 32, 512)),
        [SM, SM] + [VM] * 6,
        (VM, VM),
        (pltpu.VMEM((4, 32, 512), F32), pltpu.VMEM((128, 8), F32)),
        1_000_000,
        2_000_000,
    )(owner_rows, offset_rows, pivots.reshape(8, 128), tiles, dense_slab, *far)

    def hop(mask):
        pairs = [(r * 32 + c, c * 32 + (r ^ mask) * 4 + (r & 3)) for r in range(8) for c in range(8)]
        return lax.ppermute(left, ROWS, pairs)

    def spread(value, mask):
        return lax.ppermute(value, "col", [(z * 4 + (z & 3), (z ^ mask) * 4 + (z & 3)) for z in range(8)])

    def over_col(value, mask):
        return lax.ppermute(value, "col", [(c, c ^ mask) for c in range(32)])

    def over_row(value, mask):
        return lax.ppermute(value, "row", [(r, r ^ mask) for r in range(8)])

    pair = jnp.stack([hop(0), hop(4)])
    across = jnp.stack([piece, over_row(piece, 1)])
    got = jnp.concatenate([across] + [over_row(across, 2 * k) for k in range(1, 4)])
    left_a = (pair + spread(pair, 1)) + (spread(pair, 2) + spread(pair, 3))
    left_b = over_col(left_a, 1)
    left_c = over_col(left_a, 2)
    left_d = over_col(left_c, 1)
    full = shape(512, 512, kind=F32)
    base = call(base_kernel, full, [SM, SM, VM, VM], VM, (), 1_000_000, 3_000_000)(
        owner_rows, offset_rows, dense_slab, tiles
    )
    total = call(middle_kernel, full, [VM] * 5, VM, (), 400_000_000, 4_000_000)(base, got, left_a, left_b, left_c)
    parts = (pltpu.VMEM((512, 512), F32), pltpu.SemaphoreType.DMA((4,)))
    return call(last_kernel, full, [VM] * 3, HB, parts, 135_000_000, 3_000_000)(total, got, left_d)


def solution(mesh):
    placed = (
        P("row", "col", None, None),
        P("row", "col", None, None),
        P("row", "col"),
        P(None, "col", None),
        P(None, "col", None),
        P("row", "col"),
        P(),
    )
    return jax.shard_map(
        body, mesh=mesh, in_specs=placed, out_specs=P("row", "col"), check_vma=False
    )
```
